32 devices in a mesh: seq: 8 (over y, x, core), head: 4 (over z).
Axes of the slice: x: 2, y: 2, z: 4, core: 2. Of those that a mesh axis runs over, the one named last changes fastest.
Arguments:
- ssd_input: bfloat16 [2048, 8192], P('seq', 'head'), may hold values from -6 to 6
- gate_input: bfloat16 [2048, 8192], P('seq', 'head'), may hold values from -6 to 6
- write_vectors: bfloat16 [2048, 2048], P('seq', 'head'), may hold values from -1 to 1
- read_vectors: bfloat16 [2048, 2048], P('seq', 'head'), may hold values from -6 to 6
- log_decay: float32 [2048, 128], P('seq', 'head'), may hold values from -1 to 0
- skip_gain: float32 [128], P('head'), may hold values from 0.5 to 1.5
- norm_gain: float32 [8192], P('head'), may hold values from 0.5 to 1.5
- out_weight: bfloat16 [8192, 8192], P(None, 'head'), may hold values from -0.0625 to 0.0625
- out_grad: bfloat16 [2048, 8192], P('seq', 'head'), may hold values from -6 to 6
Outputs:
- layer_out: bfloat16 [2048, 8192], P('seq', 'head')
- input_grad: bfloat16 [2048, 8192], P('seq', 'head')
- gate_grad: bfloat16 [2048, 8192], P('seq', 'head')
- write_grad: bfloat16 [2048, 2048], P('seq', 'head')
- read_grad: bfloat16 [2048, 2048], P('seq', 'head')
- decay_grad: float32 [2048, 128], P('seq', 'head')
- weight_grad: bfloat16 [8192, 8192], P('seq', 'head')
The draws below stay inside these ranges and needn't reach their ends.
All inputs are finite; a program needn't handle non-finite values.
Results may differ from the reference program's by a relative error of at most 0.018.
Values may be sent and summed in bfloat16 or wider, within the bound.
A program may use at most 192 MiB of HBM per device.

```python
import jax
import jax.numpy as jnp
from jax import lax

D = 8192
HALF_HEADS = 128
P_SIZE = 64
N = 256
G = 8
SPAN = 256
TOK_DEV = 256
SEQUENCE_TOKENS = 2048
N_SEQ = 8
N_HEAD = 4


def draw_log_decay(key, part):
    parallel_flows = jax.random.split(jax.random.fold_in(key, 17), 7)
    fast_share = 0.5
    fast_heads = jax.random.uniform(parallel_flows[0], (HALF_HEADS,)) < fast_share
    fast_rate = jax.random.uniform(parallel_flows[1], (HALF_HEADS,), minval=0.046, maxval=0.077)
    slow_rate = jax.random.uniform(parallel_flows[2], (HALF_HEADS,), minval=0.1, maxval=0.4) * (2.3026 / SEQUENCE_TOKENS)
    per_head_rate = jnp.where(fast_heads, fast_rate, slow_rate)
    jaggedness = jax.random.uniform(parallel_flows[3], (SEQUENCE_TOKENS, HALF_HEADS), minval=0.6, maxval=1.4)
    slab_scale_factor = jnp.exp(jax.random.uniform(parallel_flows[4], (SEQUENCE_TOKENS // TOK_DEV, HALF_HEADS), minval=-0.4, maxval=0.4))
    slab_scale_factor = jnp.repeat(slab_scale_factor, TOK_DEV, axis=0)
    spike_locations = jax.random.randint(parallel_flows[5], (3,), 0, SEQUENCE_TOKENS)
    spike_hit = jnp.any(jnp.arange(SEQUENCE_TOKENS)[:, None] == spike_locations[None, :], axis=1)
    spike_loss = jnp.log(jax.random.uniform(parallel_flows[6], (SEQUENCE_TOKENS, HALF_HEADS), minval=0.5, maxval=0.8))
    return (-per_head_rate[None, :] * jaggedness * slab_scale_factor + jnp.where(spike_hit[:, None], spike_loss, 0.0)).astype(jnp.float32)


def raised(drawn, own_key, source, target, shards_of, factor):
    owner, partner = [(jnp.arange(drawn.shape[axis_at]) // (drawn.shape[axis_at] // shards_of)).reshape([-1 if axis == axis_at else 1 for axis in range(drawn.ndim)]) for axis_at in (source, target)]
    chosen = jax.random.permutation(own_key, shards_of)[partner]
    strong = (owner == chosen) | (owner == (partner + shards_of // 2) % shards_of)
    return jnp.where(strong, factor * drawn, drawn)


def levels(own_key, shape, cuts, low, largest):
    loudness = 1.0
    for dim, blocks in cuts:
        draws = jax.random.uniform(jax.random.fold_in(jax.random.fold_in(own_key, 6), dim), (blocks,), jnp.float32, low / len(cuts), largest / len(cuts))
        loudness = loudness * jnp.repeat(jnp.exp(draws), shape[dim] // blocks).reshape((-1,) + (1,) * (len(shape) - 1 - dim))
    return loudness


def scatter_about(rng, shape, width, reach, cuts=(), kind=jnp.bfloat16):
    drawn = width * jax.random.normal(rng, shape, jnp.float32)
    if cuts:
        drawn = drawn * levels(rng, shape, cuts, -0.22, 0.18)
    return jnp.clip(drawn, -reach, reach).astype(kind)


def heavy_noise(own_key, dims, deviation, most, cuts, heavy, kind=jnp.bfloat16):
    result = deviation * jax.random.normal(own_key, dims, jnp.float32)
    if cuts:
        result = result * levels(own_key, dims, cuts, -0.22, 0.18)
    return jnp.clip(raised(result, jax.random.fold_in(own_key, 3), *heavy), -most, most).astype(kind)


def setup_inputs(seed: int = 0) -> dict:
    splits = jax.random.split(jax.random.key(seed), 10)
    return {
        "ssd_input": scatter_about(splits[0], (SEQUENCE_TOKENS, HALF_HEADS * P_SIZE), 1.0, 6.0, ((0, 8), (1, 4))),
        "gate_input": scatter_about(splits[1], (SEQUENCE_TOKENS, HALF_HEADS * P_SIZE), 1.0, 6.0, ((0, 8), (1, 4))),
        "write_vectors": scatter_about(splits[2], (SEQUENCE_TOKENS, G * N), (N ** -0.5), 1.0, ((0, 8), (1, 4))),
        "read_vectors": scatter_about(splits[3], (SEQUENCE_TOKENS, G * N), 1.0, 6.0, ((0, 8), (1, 4))),
        "log_decay": draw_log_decay(jax.random.fold_in(splits[9], 71), 0),
        "skip_gain": jnp.clip(0.5 + 1.0 * jax.random.uniform(splits[5], (HALF_HEADS,), jnp.float32) ** levels(splits[5], (HALF_HEADS,), ((0, 4),), -0.2, 0.2), 0.5, 1.5),
        "norm_gain": jnp.clip(0.5 + 1.0 * jax.random.uniform(splits[6], (HALF_HEADS * P_SIZE,), jnp.float32) ** levels(splits[6], (HALF_HEADS * P_SIZE,), ((0, 4),), -0.2, 0.2), 0.5, 1.5),
        "out_weight": scatter_about(splits[7], (D, HALF_HEADS * P_SIZE), (HALF_HEADS * P_SIZE) ** -0.5, 0.0625, ((1, 4),)),
        "out_grad": heavy_noise(splits[8], (SEQUENCE_TOKENS, D), 1.0, 6.0, ((0, 8), (1, 4)), (0, 1, 8, 2.0)),
    }


epsilon = 1e-05
highest = lax.Precision.HIGHEST

def block_scan(state_now, pieces):
    input_block, write_block, read_block, decay_block = pieces
    row_count = decay_block.shape[0]
    group_count, per_group = (state_now.shape[0], state_now.shape[1])
    input_heads = input_block.reshape(row_count, group_count, per_group, P_SIZE)
    write_heads = write_block.reshape(row_count, group_count, N)
    read_heads = read_block.reshape(row_count, group_count, N)
    cumulative = jnp.cumsum(decay_block, axis=0).reshape(row_count, group_count, per_group)
    by_head = jnp.transpose(cumulative, (1, 2, 0))
    causal = lax.broadcasted_iota(jnp.int32, (row_count, row_count), 0) >= lax.broadcasted_iota(jnp.int32, (row_count, row_count), 1)
    gap_table = jnp.where(causal, by_head[..., :, None] - by_head[..., None, :], 0.0)
    decay_table = jnp.where(causal, jnp.exp(gap_table), 0.0)
    scores = jnp.einsum('tgn,sgn->gts', read_heads, write_heads, precision=highest)
    weights = scores[:, None] * decay_table
    inner_sum = jnp.einsum('gkts,sgkp->tgkp', weights, input_heads, precision=highest)
    carried = jnp.einsum('tgn,gkpn->tgkp', read_heads, state_now, precision=highest)
    output = inner_sum + jnp.exp(cumulative)[..., None] * carried
    final_log = cumulative[-1]
    weighted = input_heads * jnp.exp(final_log[None] - cumulative)[..., None]
    fresh_state = jnp.einsum('sgkp,sgn->gkpn', weighted, write_heads, precision=highest)
    next_state = jnp.exp(final_log)[..., None, None] * state_now + fresh_state
    return (next_state, output.reshape(row_count, group_count * per_group * P_SIZE))

def ssd_run(inputs, writes, reading, decays, start_state):
    row_count = decays.shape[0]
    block_count = row_count // SPAN

    def in_blocks(operand):
        return operand.reshape(block_count, SPAN, operand.shape[1])
    final_state, outputs = lax.scan(block_scan, start_state, (in_blocks(inputs), in_blocks(writes), in_blocks(reading), in_blocks(decays)))
    return (outputs.reshape(row_count, outputs.shape[2]), final_state)

def gate_norm(ssd_out, inputs, gate_values, skip_gain, norm_gain):
    row_count = ssd_out.shape[0]
    head_count = skip_gain.shape[0]
    direct = (inputs.reshape(row_count, head_count, P_SIZE) * skip_gain[:, None]).reshape(row_count, head_count * P_SIZE)
    gated_vals = (ssd_out + direct) * jax.nn.silu(gate_values)
    grouped = gated_vals.reshape(row_count, -1, HALF_HEADS * P_SIZE // G)
    factor = lax.rsqrt(lax.optimization_barrier(jnp.mean(grouped * grouped, axis=2, keepdims=True)) + epsilon)
    return (grouped * factor).reshape(row_count, head_count * P_SIZE) * norm_gain

def reference(ssd_input, gate_input, write_vectors, read_vectors, log_decay, skip_gain, norm_gain, out_weight, out_grad):
    start_state = jnp.zeros((G, HALF_HEADS // G, P_SIZE, N), jnp.float32)

    def forward(inputs, gate_values, writes, reading, decays):
        ssd_out, final_state = ssd_run(inputs, writes, reading, decays, start_state)
        return gate_norm(ssd_out, inputs, gate_values, skip_gain, norm_gain)
    normed, pull_back = jax.vjp(forward, ssd_input.astype(jnp.float32), gate_input.astype(jnp.float32), write_vectors.astype(jnp.float32), read_vectors.astype(jnp.float32), log_decay)
    normed_half = normed.astype(jnp.bfloat16)
    head_width = HALF_HEADS * P_SIZE // N_HEAD
    layer_out = jnp.zeros((SEQUENCE_TOKENS, D), jnp.float32)
    for source in range(N_HEAD):
        partial_out = jnp.dot(normed_half[:, source * head_width:(source + 1) * head_width], out_weight[:, source * head_width:(source + 1) * head_width].T, preferred_element_type=jnp.float32)
        layer_out = layer_out + lax.optimization_barrier(partial_out.astype(jnp.bfloat16)).astype(jnp.float32)
    normed_grad = jnp.dot(out_grad, out_weight, preferred_element_type=jnp.float32)
    input_grad, gate_grad, write_grad, read_grad, decay_grad = pull_back(normed_grad)
    weight_grad = jnp.zeros((D, HALF_HEADS * P_SIZE), jnp.float32)
    for source in range(N_SEQ):
        partial_grad = jnp.dot(out_grad[source * TOK_DEV:(source + 1) * TOK_DEV].T, normed_half[source * TOK_DEV:(source + 1) * TOK_DEV], preferred_element_type=jnp.float32)
        weight_grad = weight_grad + lax.optimization_barrier(partial_grad.astype(jnp.bfloat16)).astype(jnp.float32)
    return (layer_out.astype(jnp.bfloat16), input_grad.astype(jnp.bfloat16), gate_grad.astype(jnp.bfloat16), write_grad.astype(jnp.bfloat16), read_grad.astype(jnp.bfloat16), decay_grad, weight_grad.astype(jnp.bfloat16))
```

```python
from functools import partial

import jax
import jax.numpy as jnp
from jax import lax
from jax.experimental import pallas as pl
from jax.experimental.pallas import tpu as pltpu
from jax.sharding import PartitionSpec as P

P_SIZE = 64
N = 256
PAIR = 2 * P_SIZE

epsilon = 1e-05
highest = lax.Precision.HIGHEST
f32 = jnp.float32
bf16 = jnp.bfloat16
VMEM_LIMIT = 56 * 1024 * 1024


def dot(a, b, ca, cb, precision=None):
    return lax.dot_general(
        a, b, (((ca,), (cb,)), ((), ())), preferred_element_type=f32, precision=precision
    )


def spread(col, j, left):
    return jnp.where(left, col[:, 2 * j : 2 * j + 1], col[:, 2 * j + 1 : 2 * j + 2])


def left_half(rows):
    return lax.broadcasted_iota(jnp.int32, (rows, PAIR), 1) < P_SIZE


def positions(rows):
    return (
        lax.broadcasted_iota(jnp.int32, (rows, rows), 0),
        lax.broadcasted_iota(jnp.int32, (rows, rows), 1),
    )


def state_kernel(x_ref, b_ref, cum_ref, out_ref, scaled):
    rows, width = x_ref.shape
    cum = cum_ref[0]
    weight = jnp.exp(cum[rows - 1 :] - cum)
    left = left_half(rows)
    for j in range(width // PAIR):
        at = slice(j * PAIR, (j + 1) * PAIR)
        scaled[:, at] = (x_ref[:, at].astype(f32) * spread(weight, j, left)).astype(bf16)
    out_ref[0] = dot(scaled[...], b_ref[...], 0, 0).astype(bf16)


def forward_kernel(
    x_ref, gate_ref, b_ref, c_ref, cum_ref, cum_t_ref, start_ref, skip_ref, gain_ref,
    y_ref, half_ref,
):
    rows, width = x_ref.shape
    cum, cum_t = cum_ref[0], cum_t_ref[0]
    grown = jnp.exp(cum)
    left = left_half(rows)
    t, s = positions(rows)
    causal = t >= s
    scores = jnp.where(causal, dot(c_ref[...], b_ref[...], 1, 1), 0.0)
    square = jnp.zeros((rows, 1), f32)
    for j in range(width // PAIR):
        at = slice(j * PAIR, (j + 1) * PAIR)
        x = x_ref[:, at]
        inner = []
        for h in (2 * j, 2 * j + 1):
            gap = jnp.minimum(cum[:, h : h + 1] - cum_t[h : h + 1, :], 0.0)
            inner.append(dot((scores * jnp.exp(gap)).astype(bf16), x, 1, 0))
        carried = dot(c_ref[...], start_ref[0, at, :], 1, 1)
        y = jnp.where(left, inner[0], inner[1]) + spread(grown, j, left) * carried
        y_ref[:, at] = y
        v = gate_ref[:, at].astype(f32)
        gated = (y + x.astype(f32) * skip_ref[:, at]) * (v / (1.0 + jnp.exp(-v)))
        square += jnp.sum(gated * gated, axis=1, keepdims=True)
    factor = lax.rsqrt(square / width + epsilon)
    for j in range(width // PAIR):
        at = slice(j * PAIR, (j + 1) * PAIR)
        v = gate_ref[:, at].astype(f32)
        u = y_ref[:, at] + x_ref[:, at].astype(f32) * skip_ref[:, at]
        gated = u * (v / (1.0 + jnp.exp(-v)))
        half_ref[:, at] = (gated * factor * gain_ref[:, at]).astype(bf16)


def norm_back_kernel(
    x_ref, gate_ref, c_ref, cum_ref, skip_ref, gain_ref, y_ref, grad_ref,
    dy_ref, gate_grad_ref, direct_ref, scaled,
):
    rows, width = x_ref.shape
    grown = jnp.exp(cum_ref[0])
    left = left_half(rows)

    def parts(at):
        v = gate_ref[:, at].astype(f32)
        sig = 1.0 / (1.0 + jnp.exp(-v))
        u = y_ref[:, at] + x_ref[:, at].astype(f32) * skip_ref[:, at]
        return v, sig, u, u * v * sig, grad_ref[:, at] * gain_ref[:, at]

    square = jnp.zeros((rows, 1), f32)
    cross = jnp.zeros((rows, 1), f32)
    for j in range(width // PAIR):
        _, _, _, gated, dn = parts(slice(j * PAIR, (j + 1) * PAIR))
        square += jnp.sum(gated * gated, axis=1, keepdims=True)
        cross += jnp.sum(gated * dn, axis=1, keepdims=True)
    factor = lax.rsqrt(square / width + epsilon)
    back = factor * factor * (cross / width)
    for j in range(width // PAIR):
        at = slice(j * PAIR, (j + 1) * PAIR)
        v, sig, u, gated, dn = parts(at)
        dgated = factor * (dn - gated * back)
        dy = dgated * (v * sig)
        dy_ref[:, at] = dy
        gate_grad_ref[:, at] = (dgated * u * (sig * (1.0 + v * (1.0 - sig)))).astype(bf16)
        scaled[:, at] = (dy * spread(grown, j, left)).astype(bf16)
    direct_ref[0] = dot(scaled[...], c_ref[...], 0, 0).astype(bf16)


def back_kernel(
    x_ref, b_ref, c_ref, cum_ref, cum_t_ref, start_ref, end_ref, skip_ref, dy_ref,
    dx_ref, db_ref, dc_ref, decay_ref, x_scaled, dy_scaled,
):
    rows, width = x_ref.shape
    heads = cum_ref.shape[2]
    cum, cum_t = cum_ref[0], cum_t_ref[0]
    grown = jnp.exp(cum)
    fading = jnp.exp(cum[rows - 1 :] - cum)
    left = left_half(rows)
    t, s = positions(rows)
    causal = t >= s
    upper = jnp.where(t <= s, 1.0, 0.0)
    before = jnp.where(s < t, 1.0, 0.0)
    upper_half = upper.astype(bf16)
    scores = jnp.where(causal, dot(c_ref[...], b_ref[...], 1, 1), 0.0)
    lane = lax.broadcasted_iota(jnp.int32, (rows, heads), 1)
    score_grad = jnp.zeros((rows, rows), f32)
    within = jnp.zeros((rows, heads), f32)
    later = jnp.zeros((rows, heads), f32)
    earlier = jnp.zeros((rows, heads), f32)
    through = jnp.zeros((1, heads), f32)
    for j in range(width // PAIR):
        at = slice(j * PAIR, (j + 1) * PAIR)
        x = x_ref[:, at]
        dy = dy_ref[:, at]
        dy_half = dy.astype(bf16)
        start, end = start_ref[0, at, :], end_ref[0, at, :]
        dy_grown = dy * spread(grown, j, left)
        x_faded = x.astype(f32) * spread(fading, j, left)
        x_scaled[:, at] = x_faded.astype(bf16)
        dy_scaled[:, at] = dy_grown.astype(bf16)
        from_start = dy_grown * dot(c_ref[...], start, 1, 1)
        to_end = dot(b_ref[...], end, 1, 1)
        from_end = x_faded * to_end
        crossing = start.astype(f32) * end.astype(f32)
        inner = []
        for i in range(2):
            h = 2 * j + i
            mine = left if i == 0 else ~left
            own = lane == h
            gap = jnp.minimum(cum[:, h : h + 1] - cum_t[h : h + 1, :], 0.0)
            table = jnp.exp(gap)
            weights = scores * table
            pair_grad = dot(jnp.where(mine, dy_half, jnp.zeros_like(dy_half)), x, 1, 1)
            score_grad += pair_grad * table
            inner.append(dot(weights.astype(bf16), dy_half, 0, 0))
            summed = dot(upper_half, (pair_grad * weights).astype(bf16), 1, 0)
            within += jnp.where(own, jnp.sum(summed * before, axis=1, keepdims=True), 0.0)
            later += jnp.where(
                own, jnp.sum(jnp.where(mine, from_start, 0.0), axis=1, keepdims=True), 0.0
            )
            earlier += jnp.where(
                own, jnp.sum(jnp.where(mine, from_end, 0.0), axis=1, keepdims=True), 0.0
            )
            part = crossing[i * P_SIZE : (i + 1) * P_SIZE]
            total = jnp.sum(jnp.sum(part, axis=0, keepdims=True), axis=1, keepdims=True)
            through += jnp.where(own[:1], total, 0.0)
        dx = jnp.where(left, inner[0], inner[1]) + spread(fading, j, left) * to_end
        dx_ref[:, at] = (dx + dy * skip_ref[:, at]).astype(bf16)
    score_half = jnp.where(causal, score_grad, 0.0).astype(bf16)
    dc = dot(score_half, b_ref[...], 1, 0) + dot(dy_scaled[...], start_ref[0], 1, 0)
    db = dot(score_half, c_ref[...], 0, 0) + dot(x_scaled[...], end_ref[0], 1, 0)
    dc_ref[...] = dc.astype(bf16)
    db_ref[...] = db.astype(bf16)
    decay_ref[0] = (
        within
        + dot(upper, later, 1, 0, highest)
        + dot(before, earlier, 1, 0, highest)
        + jnp.exp(cum[rows - 1 :]) * through
    )


def per_device(
    ssd_input, gate_input, write_vectors, read_vectors, log_decay, skip_gain, norm_gain,
    out_weight, out_grad,
):
    rows, head_count = log_decay.shape
    groups = write_vectors.shape[1] // N
    heads = head_count // groups
    width = heads * P_SIZE
    place = lax.axis_index("seq")
    slabs = lax.axis_size("seq")

    feature = pl.BlockSpec((rows, width), lambda g: (0, g))
    vector = pl.BlockSpec((rows, N), lambda g: (0, g))
    gain = pl.BlockSpec((1, width), lambda g: (0, g))
    by_pos = pl.BlockSpec((1, rows, heads), lambda g: (g, 0, 0))
    by_head = pl.BlockSpec((1, heads, rows), lambda g: (g, 0, 0))
    state = pl.BlockSpec((1, width, N), lambda g: (g, 0, 0))
    features = (rows, groups * width)
    states = jax.ShapeDtypeStruct((groups, width, N), bf16)
    scratch = pltpu.VMEM((rows, width), bf16)

    def call(body, flops, in_specs, out_specs, out_shape, scratch_shapes=()):
        return pl.pallas_call(
            body,
            grid=(groups,),
            in_specs=in_specs,
            out_specs=out_specs,
            out_shape=out_shape,
            scratch_shapes=scratch_shapes,
            compiler_params=pltpu.CompilerParams(vmem_limit_bytes=VMEM_LIMIT),
            cost_estimate=pl.CostEstimate(
                flops=flops, bytes_accessed=8 << 20, transcendentals=1 << 20
            ),
        )

    full_grad = lax.all_gather(out_grad, "head", axis=1, tiled=True)

    t, s = positions(rows)
    cumulative = jnp.dot(jnp.where(t >= s, 1.0, 0.0), log_decay, precision=highest)
    cum = cumulative.reshape(rows, groups, heads).transpose(1, 0, 2)
    cum_t = cum.transpose(0, 2, 1)
    skip = jnp.repeat(skip_gain, P_SIZE)[None]
    gain_row = norm_gain[None]

    own_state = call(
        state_kernel, 1 << 30, [feature, vector, by_pos], state, states, [scratch]
    )(ssd_input, write_vectors, cum)

    totals = lax.all_gather(cumulative[rows - 1], "seq")
    slab = jnp.arange(slabs)
    j, i = slab[:, None, None], slab[None, :, None]
    between = (j < i) & (i < place)
    after = (place < i) & (i < j)
    log_before = jnp.sum(jnp.where(between, totals[None], 0.0), axis=1)
    log_after = jnp.sum(jnp.where(after, totals[None], 0.0), axis=1)
    share_before = jnp.where(slab[:, None] < place, jnp.exp(log_before), 0.0)
    share_after = jnp.where(slab[:, None] > place, jnp.exp(log_after), 0.0)

    def joined(own, share):
        every = lax.all_gather(own, "seq").reshape(slabs, head_count, P_SIZE, N)
        total = jnp.sum(every.astype(f32) * share[:, :, None, None], axis=0)
        return total.astype(bf16).reshape(groups, width, N)

    start_state = joined(own_state, share_before)
    ssd_out, normed_half = call(
        forward_kernel,
        4 << 30,
        [feature, feature, vector, vector, by_pos, by_head, state, gain, gain],
        [feature, feature],
        [jax.ShapeDtypeStruct(features, f32), jax.ShapeDtypeStruct(features, bf16)],
    )(ssd_input, gate_input, write_vectors, read_vectors, cum, cum_t, start_state, skip, gain_row)

    partial_out = jnp.einsum(
        "th,dh->td", normed_half, out_weight, preferred_element_type=f32
    )
    layer_out = lax.psum_scatter(
        partial_out.astype(bf16), "head", scatter_dimension=1, tiled=True
    )
    normed_all = lax.all_gather(normed_half, "seq", axis=0, tiled=True)
    grad_rows = lax.all_to_all(full_grad, "seq", split_axis=1, concat_axis=0, tiled=True)

    normed_grad = jnp.dot(full_grad, out_weight, preferred_element_type=f32)
    ssd_grad, gate_grad, direct = call(
        norm_back_kernel,
        1 << 30,
        [feature, feature, vector, by_pos, gain, gain, feature, feature],
        [feature, feature, state],
        [jax.ShapeDtypeStruct(features, f32), jax.ShapeDtypeStruct(features, bf16), states],
        [scratch],
    )(ssd_input, gate_input, read_vectors, cum, skip, gain_row, ssd_out, normed_grad)
    end_grad = joined(direct, share_after)

    vectors = jax.ShapeDtypeStruct((rows, groups * N), bf16)
    input_grad, write_grad, read_grad, decay = call(
        back_kernel,
        8 << 30,
        [feature, vector, vector, by_pos, by_head, state, state, gain, feature],
        [feature, vector, vector, by_pos],
        [
            jax.ShapeDtypeStruct(features, bf16),
            vectors,
            vectors,
            jax.ShapeDtypeStruct((groups, rows, heads), f32),
        ],
        [scratch, scratch],
    )(
        ssd_input, write_vectors, read_vectors, cum, cum_t, start_state, end_grad, skip, ssd_grad
    )
    decay_grad = decay.transpose(1, 0, 2).reshape(rows, head_count)

    weight_grad = jnp.einsum(
        "td,th->dh", grad_rows, normed_all, preferred_element_type=f32
    ).astype(bf16)
    return (layer_out, input_grad, gate_grad, write_grad, read_grad, decay_grad, weight_grad)


def solution(mesh):
    both = P("seq", "head")
    return jax.shard_map(
        per_device,
        mesh=mesh,
        in_specs=(both, both, both, both, both, P("head"), P("head"), P(None, "head"), both),
        out_specs=(both,) * 7,
        check_vma=False,
    )
```

```python
from functools import partial

import jax
import jax.numpy as jnp
from jax import lax
from jax.experimental import pallas as pl
from jax.experimental.pallas import tpu as pltpu
from jax.sharding import PartitionSpec as P

P_SIZE = 64
N = 256
PAIR = 2 * P_SIZE

epsilon = 1e-05
highest = lax.Precision.HIGHEST
f32 = jnp.float32
bf16 = jnp.bfloat16
VMEM_LIMIT = 56 * 1024 * 1024


def dot(a, b, ca, cb, precision=None):
    return lax.dot_general(
        a, b, (((ca,), (cb,)), ((), ())), preferred_element_type=f32, precision=precision
    )


def spread(col, j, left):
    return jnp.where(left, col[:, 2 * j : 2 * j + 1], col[:, 2 * j + 1 : 2 * j + 2])


def left_half(rows):
    return lax.broadcasted_iota(jnp.int32, (rows, PAIR), 1) < P_SIZE


def positions(rows):
    return (
        lax.broadcasted_iota(jnp.int32, (rows, rows), 0),
        lax.broadcasted_iota(jnp.int32, (rows, rows), 1),
    )


def state_kernel(x_ref, b_ref, cum_ref, out_ref, scaled):
    rows, width = x_ref.shape
    cum = cum_ref[0]
    weight = jnp.exp(cum[rows - 1 :] - cum)
    left = left_half(rows)
    for j in range(width // PAIR):
        at = slice(j * PAIR, (j + 1) * PAIR)
        scaled[:, at] = (x_ref[:, at].astype(f32) * spread(weight, j, left)).astype(bf16)
    out_ref[0] = dot(scaled[...], b_ref[...], 0, 0).astype(bf16)


def forward_kernel(
    x_ref, gate_ref, b_ref, c_ref, cum_ref, cum_t_ref, start_ref, skip_ref, gain_ref,
    y_ref, half_ref,
):
    rows, width = x_ref.shape
    cum, cum_t = cum_ref[0], cum_t_ref[0]
    grown = jnp.exp(cum)
    left = left_half(rows)
    t, s = positions(rows)
    causal = t >= s
    scores = jnp.where(causal, dot(c_ref[...], b_ref[...], 1, 1), 0.0)
    square = jnp.zeros((rows, 1), f32)
    for j in range(width // PAIR):
        at = slice(j * PAIR, (j + 1) * PAIR)
        x = x_ref[:, at]
        inner = []
        for h in (2 * j, 2 * j + 1):
            gap = jnp.minimum(cum[:, h : h + 1] - cum_t[h : h + 1, :], 0.0)
            inner.append(dot((scores * jnp.exp(gap)).astype(bf16), x, 1, 0))
        carried = dot(c_ref[...], start_ref[0, at, :], 1, 1)
        y = jnp.where(left, inner[0], inner[1]) + spread(grown, j, left) * carried
        y_ref[:, at] = y
        v = gate_ref[:, at].astype(f32)
        gated = (y + x.astype(f32) * skip_ref[:, at]) * (v / (1.0 + jnp.exp(-v)))
        square += jnp.sum(gated * gated, axis=1, keepdims=True)
    factor = lax.rsqrt(square / width + epsilon)
    for j in range(width // PAIR):
        at = slice(j * PAIR, (j + 1) * PAIR)
        v = gate_ref[:, at].astype(f32)
        u = y_ref[:, at] + x_ref[:, at].astype(f32) * skip_ref[:, at]
        gated = u * (v / (1.0 + jnp.exp(-v)))
        half_ref[:, at] = (gated * factor * gain_ref[:, at]).astype(bf16)


def norm_back_kernel(
    x_ref, gate_ref, c_ref, cum_ref, skip_ref, gain_ref, y_ref, grad_ref,
    dy_ref, gate_grad_ref, direct_ref, scaled,
):
    rows, width = x_ref.shape
    grown = jnp.exp(cum_ref[0])
    left = left_half(rows)

    def parts(at):
        v = gate_ref[:, at].astype(f32)
        sig = 1.0 / (1.0 + jnp.exp(-v))
        u = y_ref[:, at] + x_ref[:, at].astype(f32) * skip_ref[:, at]
        return v, sig, u, u * v * sig, grad_ref[:, at] * gain_ref[:, at]

    square = jnp.zeros((rows, 1), f32)
    cross = jnp.zeros((rows, 1), f32)
    for j in range(width // PAIR):
        _, _, _, gated, dn = parts(slice(j * PAIR, (j + 1) * PAIR))
        square += jnp.sum(gated * gated, axis=1, keepdims=True)
        cross += jnp.sum(gated * dn, axis=1, keepdims=True)
    factor = lax.rsqrt(square / width + epsilon)
    back = factor * factor * (cross / width)
    for j in range(width // PAIR):
        at = slice(j * PAIR, (j + 1) * PAIR)
        v, sig, u, gated, dn = parts(at)
        dgated = factor * (dn - gated * back)
        dy = dgated * (v * sig)
        dy_ref[:, at] = dy
        gate_grad_ref[:, at] = (dgated * u * (sig * (1.0 + v * (1.0 - sig)))).astype(bf16)
        scaled[:, at] = (dy * spread(grown, j, left)).astype(bf16)
    direct_ref[0] = dot(scaled[...], c_ref[...], 0, 0).astype(bf16)


def back_kernel(
    x_ref, b_ref, c_ref, cum_ref, cum_t_ref, start_ref, end_ref, skip_ref, dy_ref,
    dx_ref, db_ref, dc_ref, decay_ref, x_scaled, dy_scaled,
):
    rows, width = x_ref.shape
    heads = cum_ref.shape[2]
    cum, cum_t = cum_ref[0], cum_t_ref[0]
    grown = jnp.exp(cum)
    fading = jnp.exp(cum[rows - 1 :] - cum)
    left = left_half(rows)
    t, s = positions(rows)
    causal = t >= s
    upper = jnp.where(t <= s, 1.0, 0.0)
    before = jnp.where(s < t, 1.0, 0.0)
    upper_half = upper.astype(bf16)
    scores = jnp.where(causal, dot(c_ref[...], b_ref[...], 1, 1), 0.0)
    lane = lax.broadcasted_iota(jnp.int32, (rows, heads), 1)
    score_grad = jnp.zeros((rows, rows), f32)
    within = jnp.zeros((rows, heads), f32)
    later = jnp.zeros((rows, heads), f32)
    earlier = jnp.zeros((rows, heads), f32)
    through = jnp.zeros((1, heads), f32)
    for j in range(width // PAIR):
        at = slice(j * PAIR, (j + 1) * PAIR)
        x = x_ref[:, at]
        dy = dy_ref[:, at]
        dy_half = dy.astype(bf16)
        start, end = start_ref[0, at, :], end_ref[0, at, :]
        dy_grown = dy * spread(grown, j, left)
        x_faded = x.astype(f32) * spread(fading, j, left)
        x_scaled[:, at] = x_faded.astype(bf16)
        dy_scaled[:, at] = dy_grown.astype(bf16)
        from_start = dy_grown * dot(c_ref[...], start, 1, 1)
        to_end = dot(b_ref[...], end, 1, 1)
        from_end = x_faded * to_end
        crossing = start.astype(f32) * end.astype(f32)
        inner = []
        for i in range(2):
            h = 2 * j + i
            mine = left if i == 0 else ~left
            own = lane == h
            gap = jnp.minimum(cum[:, h : h + 1] - cum_t[h : h + 1, :], 0.0)
            table = jnp.exp(gap)
            weights = scores * table
            pair_grad = dot(jnp.where(mine, dy_half, jnp.zeros_like(dy_half)), x, 1, 1)
            score_grad += pair_grad * table
            inner.append(dot(weights.astype(bf16), dy_half, 0, 0))
            summed = dot(upper_half, (pair_grad * weights).astype(bf16), 1, 0)
            within += jnp.where(own, jnp.sum(summed * before, axis=1, keepdims=True), 0.0)
            later += jnp.where(
                own, jnp.sum(jnp.where(mine, from_start, 0.0), axis=1, keepdims=True), 0.0
            )
            earlier += jnp.where(
                own, jnp.sum(jnp.where(mine, from_end, 0.0), axis=1, keepdims=True), 0.0
            )
            part = crossing[i * P_SIZE : (i + 1) * P_SIZE]
            total = jnp.sum(jnp.sum(part, axis=0, keepdims=True), axis=1, keepdims=True)
            through += jnp.where(own[:1], total, 0.0)
        dx = jnp.where(left, inner[0], inner[1]) + spread(fading, j, left) * to_end
        dx_ref[:, at] = (dx + dy * skip_ref[:, at]).astype(bf16)
    score_half = jnp.where(causal, score_grad, 0.0).astype(bf16)
    dc = dot(score_half, b_ref[...], 1, 0) + dot(dy_scaled[...], start_ref[0], 1, 0)
    db = dot(score_half, c_ref[...], 0, 0) + dot(x_scaled[...], end_ref[0], 1, 0)
    dc_ref[...] = dc.astype(bf16)
    db_ref[...] = db.astype(bf16)
    decay_ref[0] = (
        within
        + dot(upper, later, 1, 0, highest)
        + dot(before, earlier, 1, 0, highest)
        + jnp.exp(cum[rows - 1 :]) * through
    )


def per_device(
    ssd_input, gate_input, write_vectors, read_vectors, log_decay, skip_gain, norm_gain,
    out_weight, out_grad,
):
    rows, head_count = log_decay.shape
    groups = write_vectors.shape[1] // N
    heads = head_count // groups
    width = heads * P_SIZE
    place = lax.axis_index("seq")
    slabs = lax.axis_size("seq")

    feature = pl.BlockSpec((rows, width), lambda g: (0, g))
    vector = pl.BlockSpec((rows, N), lambda g: (0, g))
    gain = pl.BlockSpec((1, width), lambda g: (0, g))
    by_pos = pl.BlockSpec((1, rows, heads), lambda g: (g, 0, 0))
    by_head = pl.BlockSpec((1, heads, rows), lambda g: (g, 0, 0))
    state = pl.BlockSpec((1, width, N), lambda g: (g, 0, 0))
    features = (rows, groups * width)
    states = jax.ShapeDtypeStruct((groups, width, N), bf16)
    scratch = pltpu.VMEM((rows, width), bf16)

    def call(body, flops, in_specs, out_specs, out_shape, scratch_shapes=()):
        return pl.pallas_call(
            body,
            grid=(groups,),
            in_specs=in_specs,
            out_specs=out_specs,
            out_shape=out_shape,
            scratch_shapes=scratch_shapes,
            compiler_params=pltpu.CompilerParams(vmem_limit_bytes=VMEM_LIMIT),
            cost_estimate=pl.CostEstimate(
                flops=flops, bytes_accessed=8 << 20, transcendentals=1 << 20
            ),
        )

    full_grad = lax.all_gather(out_grad, "head", axis=1, tiled=True)
    grad_rows = lax.all_to_all(full_grad, "seq", split_axis=1, concat_axis=0, tiled=True)

    t, s = positions(rows)
    cumulative = jnp.dot(jnp.where(t >= s, 1.0, 0.0), log_decay, precision=highest)
    cum = cumulative.reshape(rows, groups, heads).transpose(1, 0, 2)
    cum_t = cum.transpose(0, 2, 1)
    skip = jnp.repeat(skip_gain, P_SIZE)[None]
    gain_row = norm_gain[None]

    own_state = call(
        state_kernel, 1 << 30, [feature, vector, by_pos], state, states, [scratch]
    )(ssd_input, write_vectors, cum)

    def traded(value, step):
        return lax.ppermute(value, "seq", [(i, i ^ step) for i in range(slabs)])

    own_log = cumulative[rows - 1]
    steps = [1 << k for k in range(1, slabs.bit_length() - 1)]
    pair_log = traded(own_log, 1)
    block_log = own_log + pair_log
    block_logs = []
    for step in steps:
        other = traded(block_log, step)
        block_logs.append((block_log, other))
        block_log = block_log + other
    odd = place & 1
    half_heads = head_count // 2

    def my_half(value):
        return lax.dynamic_slice_in_dim(value, odd * half_heads, half_heads, 0)

    def decayed(log):
        return jnp.exp(log)[:, None, None]

    def joined(own, backwards):
        def is_later(step):
            return ((place & step) != 0) != backwards

        own = own.reshape(head_count, P_SIZE, N)
        pair = traded(own, 1)
        later = is_later(1)
        mine, its = my_half(own).astype(f32), my_half(pair).astype(f32)
        total = jnp.where(
            later,
            decayed(my_half(own_log)) * its + mine,
            decayed(my_half(pair_log)) * mine + its,
        ).astype(bf16)
        entering = jnp.zeros_like(total)
        entering_log = jnp.zeros((half_heads,), f32)
        for step, (log, other_log) in zip(steps, block_logs):
            other = traded(total, step)
            after = is_later(step)
            log, other_log = my_half(log), my_half(other_log)
            mine, its = total.astype(f32), other.astype(f32)
            entering = jnp.where(
                after, decayed(entering_log) * its + entering.astype(f32), entering.astype(f32)
            ).astype(bf16)
            entering_log = jnp.where(after, entering_log + other_log, entering_log)
            total = jnp.where(
                after, decayed(log) * its + mine, decayed(other_log) * mine + its
            ).astype(bf16)
        other = traded(entering, 1)
        whole = jnp.where(
            odd == 0,
            jnp.concatenate([entering, other]),
            jnp.concatenate([other, entering]),
        ).astype(f32)
        whole = jnp.where(later, decayed(pair_log) * whole + pair.astype(f32), whole)
        return whole.astype(bf16).reshape(groups, width, N)

    start_state = joined(own_state, False)
    ssd_out, normed_half = call(
        forward_kernel,
        4 << 30,
        [feature, feature, vector, vector, by_pos, by_head, state, gain, gain],
        [feature, feature],
        [jax.ShapeDtypeStruct(features, f32), jax.ShapeDtypeStruct(features, bf16)],
    )(ssd_input, gate_input, write_vectors, read_vectors, cum, cum_t, start_state, skip, gain_row)

    partial_out = jnp.einsum(
        "th,dh->td", normed_half, out_weight, preferred_element_type=f32
    )
    layer_out = lax.psum_scatter(
        partial_out.astype(bf16), "head", scatter_dimension=1, tiled=True
    )
    normed_all = lax.all_gather(normed_half, "seq", axis=0, tiled=True)

    normed_grad = jnp.dot(full_grad, out_weight, preferred_element_type=f32)
    ssd_grad, gate_grad, direct = call(
        norm_back_kernel,
        1 << 30,
        [feature, feature, vector, by_pos, gain, gain, feature, feature],
        [feature, feature, state],
        [jax.ShapeDtypeStruct(features, f32), jax.ShapeDtypeStruct(features, bf16), states],
        [scratch],
    )(ssd_input, gate_input, read_vectors, cum, skip, gain_row, ssd_out, normed_grad)
    end_grad = joined(direct, True)

    vectors = jax.ShapeDtypeStruct((rows, groups * N), bf16)
    input_grad, write_grad, read_grad, decay = call(
        back_kernel,
        8 << 30,
        [feature, vector, vector, by_pos, by_head, state, state, gain, feature],
        [feature, vector, vector, by_pos],
        [
            jax.ShapeDtypeStruct(features, bf16),
            vectors,
            vectors,
            jax.ShapeDtypeStruct((groups, rows, heads), f32),
        ],
        [scratch, scratch],
    )(
        ssd_input, write_vectors, read_vectors, cum, cum_t, start_state, end_grad, skip, ssd_grad
    )
    decay_grad = decay.transpose(1, 0, 2).reshape(rows, head_count)

    weight_grad = jnp.einsum(
        "td,th->dh", grad_rows, normed_all, preferred_element_type=f32
    ).astype(bf16)
    return (layer_out, input_grad, gate_grad, write_grad, read_grad, decay_grad, weight_grad)


def solution(mesh):
    both = P("seq", "head")
    return jax.shard_map(
        per_device,
        mesh=mesh,
        in_specs=(both, both, both, both, both, P("head"), P("head"), P(None, "head"), both),
        out_specs=(both,) * 7,
        check_vma=False,
    )
```

```python
from functools import partial

import jax
import jax.numpy as jnp
from jax import lax
from jax.experimental import pallas as pl
from jax.experimental.pallas import tpu as pltpu
from jax.sharding import PartitionSpec as P

P_SIZE = 64
N = 256
PAIR = 2 * P_SIZE

epsilon = 1e-05
highest = lax.Precision.HIGHEST
f32 = jnp.float32
bf16 = jnp.bfloat16
VMEM_LIMIT = 56 * 1024 * 1024


def dot(a, b, ca, cb, precision=None):
    return lax.dot_general(
        a, b, (((ca,), (cb,)), ((), ())), preferred_element_type=f32, precision=precision
    )


def spread(col, j, left):
    return jnp.where(left, col[:, 2 * j : 2 * j + 1], col[:, 2 * j + 1 : 2 * j + 2])


def left_half(rows):
    return lax.broadcasted_iota(jnp.int32, (rows, PAIR), 1) < P_SIZE


def positions(rows):
    return (
        lax.broadcasted_iota(jnp.int32, (rows, rows), 0),
        lax.broadcasted_iota(jnp.int32, (rows, rows), 1),
    )


def state_kernel(x_ref, b_ref, cum_ref, out_ref, scaled):
    rows, width = x_ref.shape
    cum = cum_ref[0]
    weight = jnp.exp(cum[rows - 1 :] - cum)
    left = left_half(rows)
    for j in range(width // PAIR):
        at = slice(j * PAIR, (j + 1) * PAIR)
        scaled[:, at] = (x_ref[:, at].astype(f32) * spread(weight, j, left)).astype(bf16)
    out_ref[0] = dot(scaled[...], b_ref[...], 0, 0).astype(bf16)


def forward_kernel(
    x_ref, gate_ref, b_ref, c_ref, cum_ref, cum_t_ref, start_ref, skip_ref, gain_ref,
    y_ref, half_ref,
):
    rows, width = x_ref.shape
    cum, cum_t = cum_ref[0], cum_t_ref[0]
    grown = jnp.exp(cum)
    left = left_half(rows)
    t, s = positions(rows)
    causal = t >= s
    scores = jnp.where(causal, dot(c_ref[...], b_ref[...], 1, 1), 0.0)
    square = jnp.zeros((rows, 1), f32)
    for j in range(width // PAIR):
        at = slice(j * PAIR, (j + 1) * PAIR)
        x = x_ref[:, at]
        inner = []
        for h in (2 * j, 2 * j + 1):
            gap = jnp.minimum(cum[:, h : h + 1] - cum_t[h : h + 1, :], 0.0)
            inner.append(dot((scores * jnp.exp(gap)).astype(bf16), x, 1, 0))
        carried = dot(c_ref[...], start_ref[0, at, :], 1, 1)
        y = jnp.where(left, inner[0], inner[1]) + spread(grown, j, left) * carried
        y_ref[:, at] = y
        v = gate_ref[:, at].astype(f32)
        gated = (y + x.astype(f32) * skip_ref[:, at]) * (v / (1.0 + jnp.exp(-v)))
        square += jnp.sum(gated * gated, axis=1, keepdims=True)
    factor = lax.rsqrt(square / width + epsilon)
    for j in range(width // PAIR):
        at = slice(j * PAIR, (j + 1) * PAIR)
        v = gate_ref[:, at].astype(f32)
        u = y_ref[:, at] + x_ref[:, at].astype(f32) * skip_ref[:, at]
        gated = u * (v / (1.0 + jnp.exp(-v)))
        half_ref[:, at] = (gated * factor * gain_ref[:, at]).astype(bf16)


def norm_back_kernel(
    x_ref, gate_ref, c_ref, cum_ref, skip_ref, gain_ref, y_ref, grad_ref,
    dy_ref, gate_grad_ref, direct_ref, scaled,
):
    rows, width = x_ref.shape
    grown = jnp.exp(cum_ref[0])
    left = left_half(rows)

    def parts(at):
        v = gate_ref[:, at].astype(f32)
        sig = 1.0 / (1.0 + jnp.exp(-v))
        u = y_ref[:, at] + x_ref[:, at].astype(f32) * skip_ref[:, at]
        return v, sig, u, u * v * sig, grad_ref[:, at] * gain_ref[:, at]

    square = jnp.zeros((rows, 1), f32)
    cross = jnp.zeros((rows, 1), f32)
    for j in range(width // PAIR):
        _, _, _, gated, dn = parts(slice(j * PAIR, (j + 1) * PAIR))
        square += jnp.sum(gated * gated, axis=1, keepdims=True)
        cross += jnp.sum(gated * dn, axis=1, keepdims=True)
    factor = lax.rsqrt(square / width + epsilon)
    back = factor * factor * (cross / width)
    for j in range(width // PAIR):
        at = slice(j * PAIR, (j + 1) * PAIR)
        v, sig, u, gated, dn = parts(at)
        dgated = factor * (dn - gated * back)
        dy = dgated * (v * sig)
        dy_ref[:, at] = dy
        gate_grad_ref[:, at] = (dgated * u * (sig * (1.0 + v * (1.0 - sig)))).astype(bf16)
        scaled[:, at] = (dy * spread(grown, j, left)).astype(bf16)
    direct_ref[0] = dot(scaled[...], c_ref[...], 0, 0).astype(bf16)


def back_kernel(
    x_ref, b_ref, c_ref, cum_ref, cum_t_ref, start_ref, end_ref, skip_ref, dy_ref,
    dx_ref, db_ref, dc_ref, decay_ref, x_scaled, dy_scaled,
):
    rows, width = x_ref.shape
    heads = cum_ref.shape[2]
    cum, cum_t = cum_ref[0], cum_t_ref[0]
    grown = jnp.exp(cum)
    fading = jnp.exp(cum[rows - 1 :] - cum)
    left = left_half(rows)
    t, s = positions(rows)
    causal = t >= s
    upper = jnp.where(t <= s, 1.0, 0.0)
    before = jnp.where(s < t, 1.0, 0.0)
    upper_half = upper.astype(bf16)
    scores = jnp.where(causal, dot(c_ref[...], b_ref[...], 1, 1), 0.0)
    lane = lax.broadcasted_iota(jnp.int32, (rows, heads), 1)
    score_grad = jnp.zeros((rows, rows), f32)
    within = jnp.zeros((rows, heads), f32)
    later = jnp.zeros((rows, heads), f32)
    earlier = jnp.zeros((rows, heads), f32)
    through = jnp.zeros((1, heads), f32)
    for j in range(width // PAIR):
        at = slice(j * PAIR, (j + 1) * PAIR)
        x = x_ref[:, at]
        dy = dy_ref[:, at]
        dy_half = dy.astype(bf16)
        start, end = start_ref[0, at, :], end_ref[0, at, :]
        dy_grown = dy * spread(grown, j, left)
        x_faded = x.astype(f32) * spread(fading, j, left)
        x_scaled[:, at] = x_faded.astype(bf16)
        dy_scaled[:, at] = dy_grown.astype(bf16)
        from_start = dy_grown * dot(c_ref[...], start, 1, 1)
        to_end = dot(b_ref[...], end, 1, 1)
        from_end = x_faded * to_end
        crossing = start.astype(f32) * end.astype(f32)
        inner = []
        for i in range(2):
            h = 2 * j + i
            mine = left if i == 0 else ~left
            own = lane == h
            gap = jnp.minimum(cum[:, h : h + 1] - cum_t[h : h + 1, :], 0.0)
            table = jnp.exp(gap)
            weights = scores * table
            pair_grad = dot(jnp.where(mine, dy_half, jnp.zeros_like(dy_half)), x, 1, 1)
            score_grad += pair_grad * table
            inner.append(dot(weights.astype(bf16), dy_half, 0, 0))
            summed = dot(upper_half, (pair_grad * weights).astype(bf16), 1, 0)
            within += jnp.where(own, jnp.sum(summed * before, axis=1, keepdims=True), 0.0)
            later += jnp.where(
                own, jnp.sum(jnp.where(mine, from_start, 0.0), axis=1, keepdims=True), 0.0
            )
            earlier += jnp.where(
                own, jnp.sum(jnp.where(mine, from_end, 0.0), axis=1, keepdims=True), 0.0
            )
            part = crossing[i * P_SIZE : (i + 1) * P_SIZE]
            total = jnp.sum(jnp.sum(part, axis=0, keepdims=True), axis=1, keepdims=True)
            through += jnp.where(own[:1], total, 0.0)
        dx = jnp.where(left, inner[0], inner[1]) + spread(fading, j, left) * to_end
        dx_ref[:, at] = (dx + dy * skip_ref[:, at]).astype(bf16)
    score_half = jnp.where(causal, score_grad, 0.0).astype(bf16)
    dc = dot(score_half, b_ref[...], 1, 0) + dot(dy_scaled[...], start_ref[0], 1, 0)
    db = dot(score_half, c_ref[...], 0, 0) + dot(x_scaled[...], end_ref[0], 1, 0)
    dc_ref[...] = dc.astype(bf16)
    db_ref[...] = db.astype(bf16)
    decay_ref[0] = (
        within
        + dot(upper, later, 1, 0, highest)
        + dot(before, earlier, 1, 0, highest)
        + jnp.exp(cum[rows - 1 :]) * through
    )


def per_device(
    ssd_input, gate_input, write_vectors, read_vectors, log_decay, skip_gain, norm_gain,
    out_weight, out_grad,
):
    rows, head_count = log_decay.shape
    groups = write_vectors.shape[1] // N
    heads = head_count // groups
    width = heads * P_SIZE
    place = lax.axis_index("seq")
    slabs = lax.axis_size("seq")

    feature = pl.BlockSpec((rows, width), lambda g: (0, g))
    vector = pl.BlockSpec((rows, N), lambda g: (0, g))
    gain = pl.BlockSpec((1, width), lambda g: (0, g))
    by_pos = pl.BlockSpec((1, rows, heads), lambda g: (g, 0, 0))
    by_head = pl.BlockSpec((1, heads, rows), lambda g: (g, 0, 0))
    state = pl.BlockSpec((1, width, N), lambda g: (g, 0, 0))
    features = (rows, groups * width)
    states = jax.ShapeDtypeStruct((groups, width, N), bf16)
    scratch = pltpu.VMEM((rows, width), bf16)

    def call(body, flops, in_specs, out_specs, out_shape, scratch_shapes=()):
        return pl.pallas_call(
            body,
            grid=(groups,),
            in_specs=in_specs,
            out_specs=out_specs,
            out_shape=out_shape,
            scratch_shapes=scratch_shapes,
            compiler_params=pltpu.CompilerParams(vmem_limit_bytes=VMEM_LIMIT),
            cost_estimate=pl.CostEstimate(
                flops=flops, bytes_accessed=8 << 20, transcendentals=1 << 20
            ),
        )

    full_grad = lax.all_gather(out_grad, "head", axis=1, tiled=True)

    t, s = positions(rows)
    cumulative = jnp.dot(jnp.where(t >= s, 1.0, 0.0), log_decay, precision=highest)
    cum = cumulative.reshape(rows, groups, heads).transpose(1, 0, 2)
    cum_t = cum.transpose(0, 2, 1)
    skip = jnp.repeat(skip_gain, P_SIZE)[None]
    gain_row = norm_gain[None]

    own_state = call(
        state_kernel, 1 << 30, [feature, vector, by_pos], state, states, [scratch]
    )(ssd_input, write_vectors, cum)

    def traded(value, step):
        return lax.ppermute(value, "seq", [(i, i ^ step) for i in range(slabs)])

    own_log = cumulative[rows - 1]
    steps = [1 << k for k in range(1, slabs.bit_length() - 1)]
    pair_log = traded(own_log, 1)
    block_log = own_log + pair_log
    block_logs = []
    for step in steps:
        other = traded(block_log, step)
        block_logs.append((block_log, other))
        block_log = block_log + other
    odd = place & 1
    half_heads = head_count // 2

    def my_half(value):
        return lax.dynamic_slice_in_dim(value, odd * half_heads, half_heads, 0)

    def decayed(log):
        return jnp.exp(log)[:, None, None]

    def joined(own, backwards):
        def is_later(step):
            return ((place & step) != 0) != backwards

        own = own.reshape(head_count, P_SIZE, N)
        pair = traded(own, 1)
        later = is_later(1)
        mine, its = my_half(own).astype(f32), my_half(pair).astype(f32)
        total = jnp.where(
            later,
            decayed(my_half(own_log)) * its + mine,
            decayed(my_half(pair_log)) * mine + its,
        ).astype(bf16)
        entering = jnp.zeros_like(total)
        entering_log = jnp.zeros((half_heads,), f32)
        for step, (log, other_log) in zip(steps, block_logs):
            other = traded(total, step)
            after = is_later(step)
            log, other_log = my_half(log), my_half(other_log)
            mine, its = total.astype(f32), other.astype(f32)
            entering = jnp.where(
                after, decayed(entering_log) * its + entering.astype(f32), entering.astype(f32)
            ).astype(bf16)
            entering_log = jnp.where(after, entering_log + other_log, entering_log)
            total = jnp.where(
                after, decayed(log) * its + mine, decayed(other_log) * mine + its
            ).astype(bf16)
        other = traded(entering, 1)
        whole = jnp.where(
            odd == 0,
            jnp.concatenate([entering, other]),
            jnp.concatenate([other, entering]),
        ).astype(f32)
        whole = jnp.where(later, decayed(pair_log) * whole + pair.astype(f32), whole)
        return whole.astype(bf16).reshape(groups, width, N)

    start_state = joined(own_state, False)
    ssd_out, normed_half = call(
        forward_kernel,
        4 << 30,
        [feature, feature, vector, vector, by_pos, by_head, state, gain, gain],
        [feature, feature],
        [jax.ShapeDtypeStruct(features, f32), jax.ShapeDtypeStruct(features, bf16)],
    )(ssd_input, gate_input, write_vectors, read_vectors, cum, cum_t, start_state, skip, gain_row)

    partial_out = jnp.einsum(
        "th,dh->td", normed_half, out_weight, preferred_element_type=f32
    )
    layer_out = lax.psum_scatter(
        partial_out.astype(bf16), "head", scatter_dimension=1, tiled=True
    )
    normed_all = normed_half[None]
    for step in [1 << k for k in reversed(range(slabs.bit_length() - 1))]:
        other = traded(normed_all, step)
        upper = (place & step) != 0
        normed_all = jnp.stack(
            [jnp.where(upper, other, normed_all), jnp.where(upper, normed_all, other)], axis=1
        ).reshape(-1, *normed_half.shape)
    normed_all = normed_all.reshape(-1, normed_half.shape[1])

    normed_grad = jnp.dot(full_grad, out_weight, preferred_element_type=f32)
    ssd_grad, gate_grad, direct = call(
        norm_back_kernel,
        1 << 30,
        [feature, feature, vector, by_pos, gain, gain, feature, feature],
        [feature, feature, state],
        [jax.ShapeDtypeStruct(features, f32), jax.ShapeDtypeStruct(features, bf16), states],
        [scratch],
    )(ssd_input, gate_input, read_vectors, cum, skip, gain_row, ssd_out, normed_grad)
    end_grad = joined(direct, True)
    full_grad, end_grad = lax.optimization_barrier((full_grad, end_grad))
    grad_rows = lax.all_to_all(full_grad, "seq", split_axis=1, concat_axis=0, tiled=True)

    vectors = jax.ShapeDtypeStruct((rows, groups * N), bf16)
    input_grad, write_grad, read_grad, decay = call(
        back_kernel,
        8 << 30,
        [feature, vector, vector, by_pos, by_head, state, state, gain, feature],
        [feature, vector, vector, by_pos],
        [
            jax.ShapeDtypeStruct(features, bf16),
            vectors,
            vectors,
            jax.ShapeDtypeStruct((groups, rows, heads), f32),
        ],
        [scratch, scratch],
    )(
        ssd_input, write_vectors, read_vectors, cum, cum_t, start_state, end_grad, skip, ssd_grad
    )
    decay_grad = decay.transpose(1, 0, 2).reshape(rows, head_count)

    weight_grad = jnp.einsum(
        "td,th->dh", grad_rows, normed_all, preferred_element_type=f32
    ).astype(bf16)
    return (layer_out, input_grad, gate_grad, write_grad, read_grad, decay_grad, weight_grad)


def solution(mesh):
    both = P("seq", "head")
    return jax.shard_map(
        per_device,
        mesh=mesh,
        in_specs=(both, both, both, both, both, P("head"), P("head"), P(None, "head"), both),
        out_specs=(both,) * 7,
        check_vma=False,
    )
```
